32 devices in a mesh: row: 4 (over x, core), col: 8 (over z, y).
Axes of the slice: x: 2, y: 2, z: 4, core: 2. Of those that a mesh axis runs over, the one named last changes fastest.
Arguments:
- hidden_states: bfloat16 [4096, 3072], P(('row', 'col')), may hold values from -27 to 27
- norm_gain: float32 [3072], replicated, may hold values from 0.25 to 1.75
- gate_base: bfloat16 [3072, 8192], P('row', 'col'), may hold values from -0.109375 to 0.109375
- up_base: bfloat16 [3072, 8192], P('row', 'col'), may hold values from -0.109375 to 0.109375
- down_base: bfloat16 [8192, 3072], P('col', 'row'), may hold values from -0.0625 to 0.0625
- shrink_gu: bfloat16 [1024, 3072], P('col'), may hold values from -0.109375 to 0.109375
- expand_gu: bfloat16 [2, 512, 8192], P(None, None, 'col'), may hold values from -1.5 to 1.5
- down_shrink_maps: bfloat16 [512, 8192], P(None, 'col'), may hold values from -0.0625 to 0.0625
- down_expand_maps: bfloat16 [512, 3072], P('col'), may hold values from -1.5 to 1.5
- token_adapter: int32 [4096], P('row'), may hold values from 0 to 31, as said below
- adapter_slot: int32 [32], replicated, may hold values from 0 to 31, as said below
Outputs:
- mlp_out: bfloat16 [4096, 3072], P(('row', 'col'))
The draws below stay inside these ranges and needn't reach their ends.
Inputs may be any that keep to these rules, and one draw needn't show every extreme that they name: `token_adapter`: split the tokens into aligned blocks of 128 and groups of 8 consecutive blocks: no block has more than 16 tokens whose adapters share one owner, and in each group one owner has exactly 16 tokens in every block. `adapter_slot`: A permutation of the slots.
All inputs are finite; a program needn't handle non-finite values.
Results may differ from the reference program's by a relative error of at most 0.017.
Values may be sent and summed in bfloat16 or wider, within the bound.
A program may use at most 128 MiB of HBM per device.

```python
import math
import jax
import jax.numpy as jnp
from jax import lax

D = 3072
FF = 8192
RANK = 16
ADAPT_DEV = 4
TOK_DEV = 128
CAP = 16
OWNERS = 8
ADAPTERS = 32
ROW_TOK = 1024
TOKENS = 4096
N_ROW = 4


def slot_table(key):
    return jax.random.permutation(jax.random.fold_in(key, 101), ADAPTERS).astype(jnp.int32)


def draw_adapter_slot(key, part):
    return slot_table(key)


def draw_token_adapter(key, part):
    slot_map = slot_table(key)
    holder = jnp.argsort(slot_map).astype(jnp.int32)
    blocks = TOKENS // TOK_DEV
    groups = blocks // OWNERS
    hot_owner = jax.random.randint(jax.random.fold_in(key, 102), (groups,), 0, OWNERS)
    hot_owner = jnp.repeat(hot_owner, OWNERS)
    offset = jax.random.randint(jax.random.fold_in(key, 103), (blocks,), 0, OWNERS - 1)
    position = jnp.arange(TOK_DEV, dtype=jnp.int32)
    others = (hot_owner[:, None] + 1 + (position[None, :] + offset[:, None]) % (OWNERS - 1)) % OWNERS
    owner_of = jnp.where(position[None, :] < CAP, hot_owner[:, None], others)
    block_keys = jax.random.split(jax.random.fold_in(key, 104), blocks)
    shuffle = jax.vmap(lambda one_key: jax.random.permutation(one_key, TOK_DEV))(block_keys)
    owner_of = jnp.take_along_axis(owner_of, shuffle, axis=1)
    local_index = jax.random.randint(jax.random.fold_in(key, 105), (blocks, TOK_DEV), 0, ADAPT_DEV)
    return holder[owner_of * ADAPT_DEV + local_index].reshape(TOKENS).astype(jnp.int32)


def draw_hidden_states(key, part):
    key_base = jax.random.fold_in(key, 1)
    key_rows = jax.random.fold_in(key, 2)
    key_cols = jax.random.fold_in(key, 3)
    values = jnp.clip(jax.random.normal(key_base, (TOKENS, D), jnp.float32), -3.0, 3.0)
    row_scale = jnp.exp(jax.random.uniform(key_rows, (TOKENS, 1), jnp.float32, math.log(0.3), math.log(3.0)))
    col_scale = jnp.exp(jax.random.uniform(key_cols, (1, D), jnp.float32, math.log(0.3), math.log(3.0)))
    return (values * row_scale * col_scale).astype(jnp.bfloat16)


def steps_of(stream_key, shape, cuts, smallest, largest):
    gain = 1.0
    for axis_at, parts in cuts:
        draws = jax.random.uniform(jax.random.fold_in(jax.random.fold_in(stream_key, 6), axis_at), (parts,), jnp.float32, smallest / len(cuts), largest / len(cuts))
        gain = gain * jnp.repeat(jnp.exp(draws), shape[axis_at] // parts).reshape((-1,) + (1,) * (len(shape) - 1 - axis_at))
    return gain


def gaussian(own_key, extent, width, most, cuts=(), held_as=jnp.bfloat16):
    array = width * jax.random.normal(own_key, extent, jnp.float32)
    if cuts:
        array = array * steps_of(own_key, extent, cuts, -0.22, 0.18)
    return jnp.clip(array, -most, most).astype(held_as)


def setup_inputs(seed: int = 0) -> dict:
    arg_keys = jax.random.split(jax.random.key(seed), 12)
    hidden_states = draw_hidden_states(jax.random.fold_in(arg_keys[11], 71), 0)
    norm_gain = jnp.clip(1.0 + 0.15 * jax.random.normal(arg_keys[1], (D,), jnp.float32), 0.25, 1.75)
    gate_base = gaussian(arg_keys[2], (D, FF), D ** -0.5, 0.109375, ((0, 4), (1, 8)))
    up_base = gaussian(arg_keys[3], (D, FF), D ** -0.5, 0.109375, ((0, 4), (1, 8)))
    down_base = gaussian(arg_keys[4], (FF, D), FF ** -0.5, 0.0625, ((0, 8), (1, 4)))
    shrink_gu = gaussian(arg_keys[5], (ADAPTERS * 2 * RANK, D), D ** -0.5, 0.109375, ((0, 8),))
    expand_gu = gaussian(arg_keys[6], (2, ADAPTERS * RANK, FF), RANK ** -0.5, 1.5, ((2, 8),))
    down_shrink_maps = gaussian(arg_keys[7], (ADAPTERS * RANK, FF), FF ** -0.5, 0.0625, ((1, 8),))
    down_expand_maps = gaussian(arg_keys[8], (ADAPTERS * RANK, D), RANK ** -0.5, 1.5, ((0, 8),))
    token_adapter = draw_token_adapter(jax.random.fold_in(arg_keys[11], 71), 0)
    adapter_slot = draw_adapter_slot(jax.random.fold_in(arg_keys[11], 71), 0)
    return {"hidden_states": hidden_states, "norm_gain": norm_gain, "gate_base": gate_base, "up_base": up_base, "down_base": down_base, "shrink_gu": shrink_gu, "expand_gu": expand_gu, "down_shrink_maps": down_shrink_maps, "down_expand_maps": down_expand_maps, "token_adapter": token_adapter, "adapter_slot": adapter_slot}


eps = 1e-05

def reference(hidden_states, norm_gain, gate_base, up_base, down_base, shrink_gu, expand_gu, down_shrink_maps, down_expand_maps, token_adapter, adapter_slot):
    block_width = FF // OWNERS
    adapter_range = jnp.arange(ADAPTERS, dtype=jnp.int32)
    matches = (token_adapter[:, None] == adapter_range[None, :]).astype(jnp.int32)
    slot_ids = lax.optimization_barrier(jnp.sum(matches * adapter_slot[None, :], axis=1)).astype(jnp.int32)
    down_blocks = down_base.reshape(OWNERS, block_width, D)

    def one_block(pieces):
        states, block_slots = pieces
        values = states.astype(jnp.float32)
        scale_inv = lax.rsqrt(lax.optimization_barrier(jnp.mean(values * values, axis=-1, keepdims=True)) + eps)
        normed = (values * scale_inv * norm_gain).astype(jnp.bfloat16)
        select_mask = (block_slots[:, None] == adapter_range[None, :]).astype(jnp.float32)
        select_bf = select_mask.astype(jnp.bfloat16)
        row_total = states.shape[0]
        projected_rows = jnp.dot(normed, shrink_gu.T, preferred_element_type=jnp.float32).reshape(row_total, ADAPTERS, 2 * RANK)
        ranks_gu = lax.optimization_barrier(jnp.sum(projected_rows * select_mask[:, :, None], axis=1)).astype(jnp.bfloat16)

        def spread_rank_rows(factors):
            return (select_bf[:, :, None] * factors[:, None, :]).reshape(row_total, ADAPTERS * RANK)
        gate_sum = jnp.dot(normed, gate_base, preferred_element_type=jnp.float32) + jnp.dot(spread_rank_rows(ranks_gu[:, :RANK]), expand_gu[0], preferred_element_type=jnp.float32)
        up_sum = jnp.dot(normed, up_base, preferred_element_type=jnp.float32) + jnp.dot(spread_rank_rows(ranks_gu[:, RANK:]), expand_gu[1], preferred_element_type=jnp.float32)
        hidden_rows = (jax.nn.silu(gate_sum) * up_sum).astype(jnp.bfloat16)
        down_projector = jnp.dot(hidden_rows, down_shrink_maps.T, preferred_element_type=jnp.float32).reshape(row_total, ADAPTERS, RANK)
        down_rank_rows = lax.optimization_barrier(jnp.sum(down_projector * select_mask[:, :, None], axis=1)).astype(jnp.bfloat16)
        adapter_down_term = jnp.dot(spread_rank_rows(down_rank_rows), down_expand_maps, preferred_element_type=jnp.float32).astype(jnp.bfloat16)
        adapter_down_term = lax.optimization_barrier(adapter_down_term).astype(jnp.float32)
        hidden_blocks = jnp.transpose(hidden_rows.reshape(row_total, OWNERS, block_width), (1, 0, 2))

        def add_block(running, block_pair):
            term = jnp.dot(block_pair[0], block_pair[1], preferred_element_type=jnp.float32).astype(jnp.bfloat16)
            term = lax.optimization_barrier(term).astype(jnp.float32)
            return (running + term, None)
        down_weight_shared, unused = lax.scan(add_block, jnp.zeros((row_total, D), jnp.float32), (hidden_blocks, down_blocks))
        return (down_weight_shared + adapter_down_term).astype(jnp.bfloat16)
    outputs = lax.map(one_block, (hidden_states.reshape(N_ROW, ROW_TOK, D), slot_ids.reshape(N_ROW, ROW_TOK)))
    return outputs.reshape(TOKENS, D)
```

```python
import functools

import jax
import jax.numpy as jnp
from jax import lax
from jax.experimental import pallas as pl
from jax.experimental.pallas import tpu as pltpu
from jax.sharding import PartitionSpec as P

eps = 1e-05
MESH = pl.DeviceIdType.MESH
VMEM_BYTES = 56 * 1024 * 1024


def contract_trailing(left, right):
    return lax.dot_general(
        left, right, (((left.ndim - 1,), (1,)), ((), ())), preferred_element_type=jnp.float32
    )


def rms_normed(states, norm_gain):
    values = states.astype(jnp.float32)
    scale_inv = lax.rsqrt(jnp.mean(values * values, axis=-1, keepdims=True) + eps)
    return (values * scale_inv * norm_gain).astype(jnp.bfloat16)


def ring_col(position, n):
    half = n // 2
    return jnp.where(position < half, 2 * position, 2 * (n - 1 - position) + 1)


def ring_position(col, n):
    return jnp.where(lax.rem(col, 2) == 0, col // 2, n - 1 - col // 2)


def wrap(value, n):
    return lax.rem(value + 2 * n, n)


def signal_all(devices):
    barrier = pltpu.get_barrier_semaphore()
    for device in devices:
        pl.semaphore_signal(barrier, inc=1, device_id=device, device_id_type=MESH)
    pl.semaphore_wait(barrier, len(devices))


def gather_kernel(
    n_row,
    n_col,
    tok,
    shr,
    dex,
    gate,
    up,
    down,
    tok_o,
    shr_o,
    dex_o,
    gate_o,
    up_o,
    down_o,
    own_sem,
    ring_send,
    ring_recv,
    core_send,
    core_recv,
    x_send,
    x_recv,
    pair_send,
    pair_recv,
):
    row, col = lax.axis_index("row"), lax.axis_index("col")
    n_x = n_row // 2
    x, core = row // 2, lax.rem(row, 2)
    here = ring_position(col, n_col)
    right = (row, ring_col(wrap(here + 1, n_col), n_col))
    left = (row, ring_col(wrap(here - 1, n_col), n_col))
    twin_row = x * 2 + 1 - core
    twin = (twin_row, col)
    x_peers = [(wrap(x + k, n_x) * 2 + core, col) for k in range(1, n_x)]
    signal_all([left, right, twin] + x_peers)

    t_rows, s_rows, e_rows = tok.shape[0], shr.shape[0], dex.shape[0]
    t_half, s_half, e_half = t_rows // 2, s_rows // 4, e_rows // 4

    def rows(ref, start, count):
        return ref.at[pl.ds(pl.multiple_of(start, 16), count), :]

    def place(a, block, d, c):
        if a == 0:
            return rows(tok_o, block * t_rows + d * t_half, t_half)
        if a == 1:
            base = c * (n_col * s_rows // 2) + block * (s_rows // 2)
            return rows(shr_o, base + d * s_half, s_half)
        return rows(dex_o, block * e_rows + (2 * c + d) * e_half, e_half)

    def first(a, d):
        if a == 0:
            return rows(tok, d * t_half, t_half)
        if a == 1:
            return rows(shr, core * (s_rows // 2) + d * s_half, s_half)
        return rows(dex, (2 * core + d) * e_half, e_half)

    def weight_place(w, r):
        if w == 2:
            width = down.shape[1]
            return down_o.at[:, pl.ds(pl.multiple_of(r * width, 128), width)]
        depth = gate.shape[0]
        return rows((gate_o, up_o)[w], r * depth, depth)

    weights = (gate, up, down)

    def x_copy(w, k, source, place_row):
        return pltpu.make_async_remote_copy(
            src_ref=source,
            dst_ref=weight_place(w, place_row),
            send_sem=x_send.at[w, k - 1],
            recv_sem=x_recv.at[w, k - 1],
            device_id=x_peers[k - 1],
            device_id_type=MESH,
        )

    def pair_copy(w, k, source, place_row):
        return pltpu.make_async_remote_copy(
            src_ref=source,
            dst_ref=weight_place(w, place_row),
            send_sem=pair_send.at[w, k],
            recv_sem=pair_recv.at[w, k],
            device_id=twin,
            device_id_type=MESH,
        )

    def ring_copy(a, d, step, source, block):
        return pltpu.make_async_remote_copy(
            src_ref=source,
            dst_ref=place(a, block, d, core),
            send_sem=ring_send.at[a, d, step],
            recv_sem=ring_recv.at[a, d, step],
            device_id=(right, left)[d],
            device_id_type=MESH,
        )

    def twin_copy(a, d, step, block, c):
        piece = place(a, block, d, c)
        return pltpu.make_async_remote_copy(
            src_ref=piece,
            dst_ref=piece,
            send_sem=core_send.at[a - 1, d, step],
            recv_sem=core_recv.at[a - 1, d, step],
            device_id=twin,
            device_id_type=MESH,
        )

    def block_of(d, step):
        sign = (1, -1)[d]
        return ring_col(wrap(here - sign * (1 + step), n_col), n_col)

    sides = (0, 1)
    arrays = (0, 1, 2)
    for a in arrays:
        for d in sides:
            ring_copy(a, d, 0, first(a, d), col).start()
    for w in range(3):
        for k in range(1, n_x):
            x_copy(w, k, weights[w], row).start()
    own = [
        pltpu.make_async_copy(tok, rows(tok_o, col * t_rows, t_rows), own_sem.at[0]),
        pltpu.make_async_copy(dex, rows(dex_o, col * e_rows, e_rows), own_sem.at[1]),
    ]
    for c in range(2):
        own.append(
            pltpu.make_async_copy(
                rows(shr, c * (s_rows // 2), s_rows // 2),
                rows(shr_o, (c * n_col + col) * (s_rows // 2), s_rows // 2),
                own_sem.at[2 + c],
            )
        )
    for w in range(3):
        pair_copy(w, 0, weights[w], row).start()
        own.append(pltpu.make_async_copy(weights[w], weight_place(w, row), own_sem.at[4 + w]))
    for copy in own:
        copy.start()

    last = n_col - 2

    def ring_step(step, forward):
        for a in arrays:
            for d in sides:
                block = block_of(d, step)
                piece = place(a, block, d, core)
                ring_copy(a, d, step, piece, block).wait_recv()
                if forward:
                    ring_copy(a, d, step + 1, piece, block).start()
                if a:
                    twin_copy(a, d, step, block, core).start()

    def steps(start, stop):
        @pl.loop(start, stop)
        def _(step):
            ring_step(step, True)

    def pass_on(w):
        for k in range(1, n_x):
            source_row = wrap(x - k, n_x) * 2 + core
            piece = weight_place(w, source_row)
            x_copy(w, k, piece, source_row).wait_recv()
            pair_copy(w, k, piece, source_row).start()

    steps(0, last // 2)
    pass_on(0)
    steps(last // 2, last)
    pass_on(1)
    ring_step(last, False)
    pass_on(2)

    @pl.loop(0, last + 1)
    def _(step):
        for a in arrays:
            for d in sides:
                block = block_of(d, step)
                ring_copy(a, d, step, place(a, block, d, core), block).wait_send()
                if a:
                    twin_copy(a, d, step, block, core).wait_send()
                    twin_copy(a, d, step, block, 1 - core).wait_recv()

    for w in range(3):
        for k in range(n_x):
            if k:
                x_copy(w, k, weights[w], row).wait_send()
            source_row = wrap(x - k, n_x) * 2 + core
            pair_copy(w, k, weight_place(w, source_row), source_row).wait_send()
            twin_source = wrap(x - k, n_x) * 2 + 1 - core
            pair_copy(w, k, weight_place(w, twin_source), twin_source).wait_recv()
    for copy in own:
        copy.wait()


def gather_all(n_row, n_col, tok, shr, dex, gate, up, down):
    bf = jnp.bfloat16
    outs = [
        (n_col * tok.shape[0], tok.shape[1]),
        (n_col * shr.shape[0], shr.shape[1]),
        (n_col * dex.shape[0], dex.shape[1]),
        (n_row * gate.shape[0], gate.shape[1]),
        (n_row * up.shape[0], up.shape[1]),
        (down.shape[0], n_row * down.shape[1]),
    ]
    n_x, steps = n_row // 2, n_col - 1
    dma = pltpu.SemaphoreType.DMA
    return pl.pallas_call(
        functools.partial(gather_kernel, n_row, n_col),
        out_shape=[jax.ShapeDtypeStruct(s, bf) for s in outs],
        in_specs=[pl.BlockSpec(memory_space=pl.ANY)] * 6,
        out_specs=[pl.BlockSpec(memory_space=pl.ANY)] * 6,
        scratch_shapes=[
            dma((7,)),
            dma((3, 2, steps)),
            dma((3, 2, steps)),
            dma((2, 2, steps)),
            dma((2, 2, steps)),
            dma((3, n_x - 1)),
            dma((3, n_x - 1)),
            dma((3, n_x)),
            dma((3, n_x)),
        ],
        compiler_params=pltpu.CompilerParams(
            collective_id=0, has_side_effects=True, vmem_limit_bytes=VMEM_BYTES
        ),
        name="gather_all",
    )(tok, shr, dex, gate, up, down)


def reduce_kernel(n_col, subs, part, out, held, send_sem, recv_sem):
    row, col = lax.axis_index("row"), lax.axis_index("col")
    here = ring_position(col, n_col)
    right = (row, ring_col(wrap(here + 1, n_col), n_col))
    left = (row, ring_col(wrap(here - 1, n_col), n_col))
    signal_all([left, right])
    own = out.shape[0]
    count = own // (2 * subs)
    streams = [(d, u) for u in range(subs) for d in range(2)]

    def offset(d, u):
        return (d * subs + u) * count

    def own_part(block, d, u):
        return part.at[pl.ds(pl.multiple_of(block * own + offset(d, u), 16), count), :]

    def target(d, step):
        sign = (1, -1)[d]
        return ring_col(wrap(here - sign * (2 + step), n_col), n_col)

    def copy(d, u, step, source):
        return pltpu.make_async_remote_copy(
            src_ref=source,
            dst_ref=held.at[d, u, step],
            send_sem=send_sem.at[d, u, step],
            recv_sem=recv_sem.at[d, u, step],
            device_id=(right, left)[d],
            device_id_type=MESH,
        )

    for d, u in streams:
        copy(d, u, 0, own_part((left, right)[d][1], d, u)).start()
    last = n_col - 2

    @pl.loop(0, last)
    def _(step):
        for d, u in streams:
            slot = held.at[d, u, step]
            copy(d, u, step, slot).wait_recv()
            total = slot[...].astype(jnp.float32) + own_part(target(d, step), d, u)[...].astype(
                jnp.float32
            )
            slot[...] = total.astype(jnp.bfloat16)
            copy(d, u, step + 1, slot).start()

    for d, u in streams:
        slot = held.at[d, u, last]
        copy(d, u, last, slot).wait_recv()
        total = slot[...].astype(jnp.float32) + own_part(col, d, u)[...].astype(jnp.float32)
        out[pl.ds(offset(d, u), count), :] = total.astype(jnp.bfloat16)

    @pl.loop(0, last + 1)
    def _(step):
        for d, u in streams:
            copy(d, u, step, held.at[d, u, step]).wait_send()


def reduce_blocks(n_col, part):
    own, width = part.shape[0] // n_col, part.shape[1]
    subs = 2
    steps = n_col - 1
    dma = pltpu.SemaphoreType.DMA
    return pl.pallas_call(
        functools.partial(reduce_kernel, n_col, subs),
        out_shape=jax.ShapeDtypeStruct((own, width), jnp.bfloat16),
        in_specs=[pl.BlockSpec(memory_space=pltpu.VMEM)],
        out_specs=pl.BlockSpec(memory_space=pltpu.VMEM),
        scratch_shapes=[
            pltpu.VMEM((2, subs, steps, own // (2 * subs), width), jnp.bfloat16),
            dma((2, subs, steps)),
            dma((2, subs, steps)),
        ],
        compiler_params=pltpu.CompilerParams(
            collective_id=1, has_side_effects=True, vmem_limit_bytes=VMEM_BYTES
        ),
        name="reduce_blocks",
    )(part)


def local(
    n_row,
    n_col,
    hidden_states,
    norm_gain,
    gate_base,
    up_base,
    down_base,
    shrink_gu,
    expand_gu,
    down_shrink_maps,
    down_expand_maps,
    token_adapter,
    adapter_slot,
):
    adapter_list = adapter_slot.shape[0]
    owned = adapter_list // n_col
    rank = down_expand_maps.shape[0] // owned
    adapter_range = jnp.arange(adapter_list, dtype=jnp.int32)
    normed = rms_normed(hidden_states, norm_gain)
    matches = (token_adapter[:, None] == adapter_range[None, :]).astype(jnp.int32)
    row_slots = jnp.sum(matches * adapter_slot[None, :], axis=1)
    by_side = (
        shrink_gu.reshape(owned, 2, rank, -1).transpose(1, 0, 2, 3).reshape(shrink_gu.shape)
    )
    tokens, shrink, expand_down, gate_full, up_full, down_full = gather_all(
        n_row, n_col, normed, by_side, down_expand_maps, gate_base, up_base, down_base
    )
    ranks = adapter_list * rank
    chosen = (jnp.arange(ranks, dtype=jnp.int32) // rank)[None, :] == row_slots[:, None]

    def spread(projected):
        return jnp.where(chosen, projected, 0.0).astype(jnp.bfloat16)

    def dot(left, right):
        return jnp.dot(left, right, preferred_element_type=jnp.float32)

    gate_sum = dot(tokens, gate_full) + dot(
        spread(contract_trailing(tokens, shrink[:ranks])), expand_gu[0]
    )
    up_sum = dot(tokens, up_full) + dot(
        spread(contract_trailing(tokens, shrink[ranks:])), expand_gu[1]
    )
    hidden_rows = (jax.nn.silu(gate_sum) * up_sum).astype(jnp.bfloat16)
    down_spread = spread(contract_trailing(hidden_rows, down_shrink_maps))
    part = (dot(hidden_rows, down_full) + dot(down_spread, expand_down)).astype(jnp.bfloat16)
    return reduce_blocks(n_col, part)


def solution(mesh):
    in_specs = (
        P(("row", "col"), None),
        P(),
        P("row", "col"),
        P("row", "col"),
        P("col", "row"),
        P("col", None),
        P(None, None, "col"),
        P(None, "col"),
        P("col", None),
        P("row"),
        P(),
    )
    out_specs = P(("row", "col"), None)
    return jax.shard_map(
        functools.partial(local, mesh.shape["row"], mesh.shape["col"]),
        mesh=mesh,
        in_specs=in_specs,
        out_specs=out_specs,
        check_vma=False,
    )
```

```python
import functools

import jax
import jax.numpy as jnp
from jax import lax
from jax.experimental import pallas as pl
from jax.experimental.pallas import tpu as pltpu
from jax.sharding import PartitionSpec as P

eps = 1e-05
MESH = pl.DeviceIdType.MESH
VMEM_BYTES = 56 * 1024 * 1024


def contract_trailing(left, right):
    return lax.dot_general(
        left, right, (((left.ndim - 1,), (1,)), ((), ())), preferred_element_type=jnp.float32
    )


def rms_normed(states, norm_gain):
    values = states.astype(jnp.float32)
    scale_inv = lax.rsqrt(jnp.mean(values * values, axis=-1, keepdims=True) + eps)
    return (values * scale_inv * norm_gain).astype(jnp.bfloat16)


def ring_col(position, n):
    half = n // 2
    return jnp.where(position < half, 2 * position, 2 * (n - 1 - position) + 1)


def ring_position(col, n):
    return jnp.where(lax.rem(col, 2) == 0, col // 2, n - 1 - col // 2)


def wrap(value, n):
    return lax.rem(value + 2 * n, n)


def signal_all(devices):
    barrier = pltpu.get_barrier_semaphore()
    for device in devices:
        pl.semaphore_signal(barrier, inc=1, device_id=device, device_id_type=MESH)
    pl.semaphore_wait(barrier, len(devices))


def gather_kernel(
    n_col,
    tok,
    shr,
    dex,
    tok_o,
    shr_o,
    dex_o,
    own_sem,
    ring_send,
    ring_recv,
    core_send,
    core_recv,
):
    row, col = lax.axis_index("row"), lax.axis_index("col")
    core = lax.rem(row, 2)
    here = ring_position(col, n_col)
    right = (row, ring_col(wrap(here + 1, n_col), n_col))
    left = (row, ring_col(wrap(here - 1, n_col), n_col))
    twin = (row + 1 - 2 * core, col)
    signal_all([left, right, twin])

    t_rows, s_rows, e_rows = tok.shape[0], shr.shape[0], dex.shape[0]
    t_half, s_half, e_half = t_rows // 2, s_rows // 4, e_rows // 4

    def rows(ref, start, count):
        return ref.at[pl.ds(pl.multiple_of(start, 16), count), :]

    def place(a, block, d, c):
        if a == 0:
            return rows(tok_o, block * t_rows + d * t_half, t_half)
        if a == 1:
            base = c * (n_col * s_rows // 2) + block * (s_rows // 2)
            return rows(shr_o, base + d * s_half, s_half)
        return rows(dex_o, block * e_rows + (2 * c + d) * e_half, e_half)

    def first(a, d):
        if a == 0:
            return rows(tok, d * t_half, t_half)
        if a == 1:
            return rows(shr, core * (s_rows // 2) + d * s_half, s_half)
        return rows(dex, (2 * core + d) * e_half, e_half)

    def ring_copy(a, d, step, source, block):
        return pltpu.make_async_remote_copy(
            src_ref=source,
            dst_ref=place(a, block, d, core),
            send_sem=ring_send.at[a, d, step],
            recv_sem=ring_recv.at[a, d, step],
            device_id=(right, left)[d],
            device_id_type=MESH,
        )

    def twin_copy(a, d, step, block, c):
        piece = place(a, block, d, c)
        return pltpu.make_async_remote_copy(
            src_ref=piece,
            dst_ref=piece,
            send_sem=core_send.at[a - 1, d, step],
            recv_sem=core_recv.at[a - 1, d, step],
            device_id=twin,
            device_id_type=MESH,
        )

    def block_of(d, step):
        sign = (1, -1)[d]
        return ring_col(wrap(here - sign * (1 + step), n_col), n_col)

    sides = (0, 1)
    arrays = (0, 1, 2)
    for a in arrays:
        for d in sides:
            ring_copy(a, d, 0, first(a, d), col).start()
    own = [
        pltpu.make_async_copy(tok, rows(tok_o, col * t_rows, t_rows), own_sem.at[0]),
        pltpu.make_async_copy(dex, rows(dex_o, col * e_rows, e_rows), own_sem.at[1]),
    ]
    for c in range(2):
        own.append(
            pltpu.make_async_copy(
                rows(shr, c * (s_rows // 2), s_rows // 2),
                rows(shr_o, (c * n_col + col) * (s_rows // 2), s_rows // 2),
                own_sem.at[2 + c],
            )
        )
    for copy in own:
        copy.start()

    last = n_col - 2

    def ring_step(step, forward):
        for a in arrays:
            for d in sides:
                block = block_of(d, step)
                piece = place(a, block, d, core)
                ring_copy(a, d, step, piece, block).wait_recv()
                if forward:
                    ring_copy(a, d, step + 1, piece, block).start()
                if a:
                    twin_copy(a, d, step, block, core).start()

    @pl.loop(0, last)
    def _(step):
        ring_step(step, True)

    ring_step(last, False)

    @pl.loop(0, last + 1)
    def _(step):
        for a in arrays:
            for d in sides:
                block = block_of(d, step)
                ring_copy(a, d, step, place(a, block, d, core), block).wait_send()
                if a:
                    twin_copy(a, d, step, block, core).wait_send()
                    twin_copy(a, d, step, block, 1 - core).wait_recv()

    for copy in own:
        copy.wait()


def gather_all(n_col, tok, shr, dex):
    bf = jnp.bfloat16
    outs = [
        (n_col * tok.shape[0], tok.shape[1]),
        (n_col * shr.shape[0], shr.shape[1]),
        (n_col * dex.shape[0], dex.shape[1]),
    ]
    steps = n_col - 1
    dma = pltpu.SemaphoreType.DMA
    return pl.pallas_call(
        functools.partial(gather_kernel, n_col),
        out_shape=[jax.ShapeDtypeStruct(s, bf) for s in outs],
        in_specs=[pl.BlockSpec(memory_space=pl.ANY)] * 3,
        out_specs=[pl.BlockSpec(memory_space=pl.ANY)] * 3,
        scratch_shapes=[
            dma((4,)),
            dma((3, 2, steps)),
            dma((3, 2, steps)),
            dma((2, 2, steps)),
            dma((2, 2, steps)),
        ],
        compiler_params=pltpu.CompilerParams(
            collective_id=0, has_side_effects=True, vmem_limit_bytes=VMEM_BYTES
        ),
        name="gather_all",
    )(tok, shr, dex)


def reduce_kernel(n_col, subs, part, out, held, send_sem, recv_sem):
    row, col = lax.axis_index("row"), lax.axis_index("col")
    here = ring_position(col, n_col)
    right = (row, ring_col(wrap(here + 1, n_col), n_col))
    left = (row, ring_col(wrap(here - 1, n_col), n_col))
    signal_all([left, right])
    own = out.shape[0]
    count = own // (2 * subs)
    streams = [(d, u) for u in range(subs) for d in range(2)]

    def offset(d, u):
        return (d * subs + u) * count

    def own_part(block, d, u):
        return part.at[pl.ds(pl.multiple_of(block * own + offset(d, u), 16), count), :]

    def target(d, step):
        sign = (1, -1)[d]
        return ring_col(wrap(here - sign * (2 + step), n_col), n_col)

    def copy(d, u, step, source):
        return pltpu.make_async_remote_copy(
            src_ref=source,
            dst_ref=held.at[d, u, step],
            send_sem=send_sem.at[d, u, step],
            recv_sem=recv_sem.at[d, u, step],
            device_id=(right, left)[d],
            device_id_type=MESH,
        )

    for d, u in streams:
        copy(d, u, 0, own_part((left, right)[d][1], d, u)).start()
    last = n_col - 2

    @pl.loop(0, last)
    def _(step):
        for d, u in streams:
            slot = held.at[d, u, step]
            copy(d, u, step, slot).wait_recv()
            total = slot[...].astype(jnp.float32) + own_part(target(d, step), d, u)[...].astype(
                jnp.float32
            )
            slot[...] = total.astype(jnp.bfloat16)
            copy(d, u, step + 1, slot).start()

    for d, u in streams:
        slot = held.at[d, u, last]
        copy(d, u, last, slot).wait_recv()
        total = slot[...].astype(jnp.float32) + own_part(col, d, u)[...].astype(jnp.float32)
        out[pl.ds(offset(d, u), count), :] = total.astype(jnp.bfloat16)

    @pl.loop(0, last + 1)
    def _(step):
        for d, u in streams:
            copy(d, u, step, held.at[d, u, step]).wait_send()


def reduce_blocks(n_col, part):
    own, width = part.shape[0] // n_col, part.shape[1]
    subs = 2
    steps = n_col - 1
    dma = pltpu.SemaphoreType.DMA
    return pl.pallas_call(
        functools.partial(reduce_kernel, n_col, subs),
        out_shape=jax.ShapeDtypeStruct((own, width), jnp.bfloat16),
        in_specs=[pl.BlockSpec(memory_space=pltpu.VMEM)],
        out_specs=pl.BlockSpec(memory_space=pltpu.VMEM),
        scratch_shapes=[
            pltpu.VMEM((2, subs, steps, own // (2 * subs), width), jnp.bfloat16),
            dma((2, subs, steps)),
            dma((2, subs, steps)),
        ],
        compiler_params=pltpu.CompilerParams(
            collective_id=1, has_side_effects=True, vmem_limit_bytes=VMEM_BYTES
        ),
        name="reduce_blocks",
    )(part)


def local(
    n_col,
    hidden_states,
    norm_gain,
    gate_base,
    up_base,
    down_base,
    shrink_gu,
    expand_gu,
    down_shrink_maps,
    down_expand_maps,
    token_adapter,
    adapter_slot,
):
    adapter_list = adapter_slot.shape[0]
    owned = adapter_list // n_col
    rank = down_expand_maps.shape[0] // owned
    adapter_range = jnp.arange(adapter_list, dtype=jnp.int32)
    normed = rms_normed(hidden_states, norm_gain)
    matches = (token_adapter[:, None] == adapter_range[None, :]).astype(jnp.int32)
    row_slots = jnp.sum(matches * adapter_slot[None, :], axis=1)
    by_side = (
        shrink_gu.reshape(owned, 2, rank, -1).transpose(1, 0, 2, 3).reshape(shrink_gu.shape)
    )
    gate_full = lax.all_gather(gate_base, "row", axis=0, tiled=True)
    up_full = lax.all_gather(up_base, "row", axis=0, tiled=True)
    down_full = lax.all_gather(down_base, "row", axis=1, tiled=True)
    tokens, shrink, expand_down = gather_all(n_col, normed, by_side, down_expand_maps)
    ranks = adapter_list * rank
    chosen = (jnp.arange(ranks, dtype=jnp.int32) // rank)[None, :] == row_slots[:, None]

    def spread(projected):
        return jnp.where(chosen, projected, 0.0).astype(jnp.bfloat16)

    def dot(left, right):
        return jnp.dot(left, right, preferred_element_type=jnp.float32)

    gate_sum = dot(tokens, gate_full) + dot(
        spread(contract_trailing(tokens, shrink[:ranks])), expand_gu[0]
    )
    up_sum = dot(tokens, up_full) + dot(
        spread(contract_trailing(tokens, shrink[ranks:])), expand_gu[1]
    )
    hidden_rows = (jax.nn.silu(gate_sum) * up_sum).astype(jnp.bfloat16)
    down_spread = spread(contract_trailing(hidden_rows, down_shrink_maps))
    part = (dot(hidden_rows, down_full) + dot(down_spread, expand_down)).astype(jnp.bfloat16)
    return reduce_blocks(n_col, part)


def solution(mesh):
    in_specs = (
        P(("row", "col"), None),
        P(),
        P("row", "col"),
        P("row", "col"),
        P("col", "row"),
        P("col", None),
        P(None, None, "col"),
        P(None, "col"),
        P("col", None),
        P("row"),
        P(),
    )
    out_specs = P(("row", "col"), None)
    return jax.shard_map(
        functools.partial(local, mesh.shape["col"]),
        mesh=mesh,
        in_specs=in_specs,
        out_specs=out_specs,
        check_vma=False,
    )
```
